512 devices in a mesh: ctx: 32 (over x, y), tp: 16 (over z, core).
Axes of the slice: x: 4, y: 8, z: 8, core: 2. Of those that a mesh axis runs over, the one named last changes fastest.
Arguments:
- gate_in: bfloat16 [16384, 4096], P('ctx', 'tp'), may hold values from -6 to 6
- key_in: bfloat16 [16384, 4096], P('ctx', 'tp'), may hold values from -6 to 6
- value_in: bfloat16 [16384, 4096], P('ctx', 'tp'), may hold values from -60 to 60
- filters: bfloat16 [16384, 4096], P('ctx', 'tp'), may hold values from -1 to 1
- skip: float32 [4096], P('tp'), may hold values from -1 to 1
- gain: float32 [4096], P('tp'), may hold values from 0.1 to 1.9
Outputs:
- output: bfloat16 [16384, 4096], P('ctx', 'tp')
The draws below stay inside these ranges and needn't reach their ends.
All inputs are finite; a program needn't handle non-finite values.
Results may differ from the reference program's by a relative error of at most 0.0049.
Values may be sent and summed in bfloat16 or wider, within the bound.
No kernel may reach another device: no remote copies, remote signals or barrier semaphores. Data moves between devices by JAX's collectives and lax.ppermute only.
A program may use at most 64 MiB of HBM per device.

```python
import math
import jax
import jax.numpy as jnp
from jax import lax

TOKENS = 16384
C = 4096


def draw_value_in(key, part):
    key = jax.random.fold_in(key, 11)
    noise_key, token_key, quiet_key = jax.random.split(key, 3)
    token_scale = jnp.exp(jax.random.uniform(token_key, (TOKENS, 1), jnp.float32) * math.log(10.0))
    position = jnp.arange(C, dtype=jnp.float32)[None, :] / max(C - 1, 1)
    quiet_len = TOKENS // 4
    quiet_start = jax.random.randint(quiet_key, (), 0, TOKENS - quiet_len + 1)
    row_ids = jnp.arange(TOKENS, dtype=jnp.int32)[:, None]
    live_rows = jnp.logical_or(row_ids < quiet_start, row_ids >= quiet_start + quiet_len).astype(jnp.float32)
    noise = jax.random.truncated_normal(noise_key, -3.0, 3.0, (TOKENS, C), jnp.float32)
    spread = math.log(10.0)
    return (noise * jnp.exp(position * spread) * token_scale * 0.1 * live_rows).astype(jnp.bfloat16)


def draw_filters(key, part):
    key = jax.random.fold_in(key, 23)
    rate_key, noise_key, lag_key, slow_key, amp_key = jax.random.split(key, 5)
    lowest = 0.5 / TOKENS
    highest = 1.0 / 30.0
    noise = jax.random.truncated_normal(noise_key, -3.0, 3.0, (TOKENS, C), jnp.float32)
    rates = jnp.exp(jax.random.uniform(rate_key, (1, C), jnp.float32, math.log(lowest), math.log(highest)))
    slow_rates = jnp.exp(jax.random.uniform(slow_key, (1, C), jnp.float32, math.log(0.3 / TOKENS), math.log(1.0 / TOKENS)))
    slow_amp = jax.random.uniform(amp_key, (1, C), jnp.float32, 0.4, 0.8)
    lag_ids = jnp.arange(TOKENS, dtype=jnp.int32)
    drop_lags = jax.random.randint(lag_key, (3,), 1, TOKENS)
    drop_count = jnp.sum((lag_ids[:, None] >= drop_lags[None, :]).astype(jnp.float32), axis=1)
    drop_factor = jnp.power(0.6, drop_count)
    lag_float = lag_ids.astype(jnp.float32)[:, None]
    fast_part = jnp.sqrt(2.0 * rates) * jnp.exp(-rates * lag_float)
    slow_part = slow_amp * jnp.sqrt(2.0 * slow_rates) * jnp.exp(-slow_rates * lag_float)
    envelope = (fast_part + slow_part) * drop_factor[:, None]
    return (noise * envelope).astype(jnp.bfloat16)


def level_of(rng, extent, shards, least, high):
    def one(dim, shards_of):
        draws = jax.random.uniform(jax.random.fold_in(jax.random.fold_in(rng, 6), dim), (shards_of,), jnp.float32, least / len(shards), high / len(shards))
        return jnp.repeat(jnp.exp(draws), extent[dim] // shards_of).reshape((-1,) + (1,) * (len(extent) - dim - 1))

    loudness = one(*shards[0])
    for cut in shards[1:]:
        loudness = loudness * one(*cut)
    return loudness


def scatter_about(key, shape, scale, limit, cuts=(), held_as=jnp.bfloat16):
    entries = jax.random.normal(key, shape, jnp.float32) * scale
    if len(cuts) > 0:
        entries = level_of(key, shape, cuts, -0.22, 0.18) * entries
    return jnp.clip(entries, min=-limit, max=limit).astype(held_as)


def setup_inputs(seed: int = 0) -> dict:
    key_of = jax.random.split(jax.random.key(seed), 7)
    gate_in = scatter_about(key_of[0], (TOKENS, C), 1.0, 6.0, ((0, 32), (1, 16)))
    key_in = scatter_about(key_of[1], (TOKENS, C), 1.0, 6.0, ((0, 32), (1, 16)))
    value_in = draw_value_in(jax.random.fold_in(key_of[6], 71), 0)
    filters = draw_filters(jax.random.fold_in(key_of[6], 71), 0)
    skip = jnp.clip(jax.random.uniform(key_of[4], (C,), jnp.float32, -1.0, 1.0) * level_of(key_of[4], (C,), ((0, 16),), -0.4, 0.0), -1.0, 1.0)
    gain = jnp.clip(1.0 + 0.18 * jax.random.normal(key_of[5], (C,), jnp.float32), 0.1, 1.9)
    return dict(gate_in=gate_in, key_in=key_in, value_in=value_in, filters=filters, skip=skip, gain=gain)


def reference(gate_in, key_in, value_in, filters, skip, gain):
    mixed = (key_in.astype(jnp.float32) * value_in.astype(jnp.float32)).astype(jnp.bfloat16)
    block_width = math.gcd(C, 256)
    block_count = C // block_width
    padded_len = 2 * TOKENS

    def convolve(pair):
        signal, taps = pair
        spectrum = jnp.fft.rfft(signal.astype(jnp.float32), n=padded_len, axis=0) * jnp.fft.rfft(taps.astype(jnp.float32), n=padded_len, axis=0)
        return jnp.fft.irfft(spectrum, n=padded_len, axis=0)[:TOKENS]
    signal_blocks = mixed.reshape(TOKENS, block_count, block_width).transpose(1, 0, 2)
    tap_blocks = filters.reshape(TOKENS, block_count, block_width).transpose(1, 0, 2)
    conv = lax.map(convolve, (signal_blocks, tap_blocks))
    conv = conv.transpose(1, 0, 2).reshape(TOKENS, C)
    summed = conv + skip[None, :] * mixed.astype(jnp.float32)
    energy = lax.optimization_barrier(jnp.sum(summed * summed, axis=1))
    scale_row = lax.rsqrt(energy / C + 1e-05)
    return (gate_in.astype(jnp.float32) * summed * scale_row[:, None] * gain[None, :]).astype(jnp.bfloat16)
```

```python
import functools

import jax
import jax.numpy as jnp
from jax import lax
from jax.experimental import pallas as pl
from jax.experimental.pallas import tpu as pltpu
from jax.sharding import PartitionSpec as P

EPSILON = 1e-05
LANES = 128
GROUP = 8
PAD = 16
F32 = jnp.float32
BF16 = jnp.bfloat16


def whole(shape=None):
    return pl.BlockSpec(memory_space=pltpu.VMEM)


def flip_blocks(rows):
    parts = []
    for a in range(rows.shape[0] // LANES):
        block = rows[a * LANES : (a + 1) * LANES, :].T
        parts.append(block.reshape(block.shape[0] // GROUP, GROUP, LANES))
    return jnp.concatenate(parts, axis=1)


def pack_kernel(key_ref, value_ref, taps_ref, out_ref):
    mixed = key_ref[...].astype(F32) * value_ref[...].astype(F32)
    half = out_ref.shape[1] // 2
    out_ref[:, :half, :] = flip_blocks(mixed).astype(BF16)
    out_ref[:, half:, :] = flip_blocks(taps_ref[...].astype(F32)).astype(BF16)


def conv_kernel(recv_ref, skip_ref, out_ref, x_all, h_all, y_all, x_pad, h_pad, odd_pad, acc, toe_a, toe_b):
    owners, both, _ = recv_ref.shape
    half = both // 2
    x_all[...] = recv_ref[:, :half, :].astype(F32).reshape(owners * half, LANES)
    h_all[...] = recv_ref[:, half:, :].astype(F32).reshape(owners * half, LANES)
    x_pad[:PAD, :] = jnp.zeros((PAD, LANES), F32)
    h_pad[:8, :] = jnp.zeros((8, LANES), F32)
    odd_pad[:8, :] = jnp.zeros((8, LANES), F32)
    lane = lax.broadcasted_iota(jnp.int32, (8, LANES), 1)
    row = lax.broadcasted_iota(jnp.int32, (8, LANES), 0)
    edge = lane + row

    def toeplitz(k):
        now = jnp.broadcast_to(h_pad[8 + k : 9 + k, :], (8, LANES))
        before = jnp.broadcast_to(h_pad[7 + k : 8 + k, :], (8, LANES))
        tiles = []
        for v in range(LANES // 8):
            mixed_row = jnp.where(edge >= LANES - 8 * v, before, now)
            tiles.append(pltpu.roll(mixed_row, 8 * v, 1, stride=1, stride_axis=0))
        return jnp.concatenate(tiles, axis=0).astype(BF16)

    def channel(c, carry):
        x = x_all[pl.ds(c, LANES, stride=GROUP), :]
        x_pad[PAD:, :] = x
        h_pad[8:, :] = h_all[pl.ds(c, LANES, stride=GROUP), :]
        lhs = jnp.concatenate(
            [x_pad[PAD - b : PAD - b + LANES, :].astype(BF16) for b in range(0, 16, 2)], axis=1
        )
        for a in range(8):
            toe = (toe_a, toe_b)[a % 2]
            for b in range(0, 16, 2):
                for e in range(2):
                    toe[b // 2 * LANES : (b // 2 + 1) * LANES, e * LANES : (e + 1) * LANES] = toeplitz(
                        16 * a + b + e
                    )
            part = jnp.dot(lhs[: LANES - 16 * a, :], toe[...], preferred_element_type=F32)
            if a == 0:
                acc[...] = part
            else:
                acc[16 * a :, :] += part
        odd_pad[8:, :] = acc[:, LANES:]
        conv = acc[:, :LANES] + odd_pad[7 : 7 + LANES, :]
        y_all[pl.ds(c, LANES, stride=GROUP), :] = conv + skip_ref[c] * x
        return carry

    lax.fori_loop(0, GROUP, channel, 0)
    out_ref[...] = y_all[...].reshape(out_ref.shape).astype(BF16)


def energy_kernel(back_ref, out_ref):
    owners, rows, _ = back_ref.shape
    values = back_ref[...].astype(F32).reshape(owners, rows // GROUP, GROUP, LANES)
    total = jnp.sum(values * values, axis=0)
    own = jnp.sum(total, axis=1)
    for i in range(out_ref.shape[0]):
        out_ref[i] = own


def finish_kernel(channels, back_ref, gate_ref, energy_ref, gain_ref, out_ref):
    owners, rows, _ = back_ref.shape
    energy = jnp.sum(energy_ref[...], axis=0)
    scale = lax.rsqrt(energy / channels + EPSILON)
    values = back_ref[...].astype(F32)
    gain = gain_ref[...]
    for a in range(rows // GROUP):
        block = values[:, a * GROUP : (a + 1) * GROUP, :].reshape(owners * GROUP, LANES)
        block = (block * scale[a : a + 1, :]).T
        span = slice(a * LANES, (a + 1) * LANES)
        out_ref[span, :] = (gate_ref[span, :].astype(F32) * block * gain).astype(BF16)


def per_device(gate_in, key_in, value_in, filters, skip, gain):
    rows, channels = key_in.shape
    ctx = lax.axis_size("ctx")
    tp = lax.axis_size("tp")
    blocks = rows // LANES
    here = blocks * GROUP
    params = pltpu.CompilerParams(vmem_limit_bytes=32 * 1024 * 1024)
    packed = pl.pallas_call(
        pack_kernel,
        out_shape=jax.ShapeDtypeStruct((ctx, 2 * here, LANES), BF16),
        in_specs=[whole()] * 3,
        out_specs=whole(),
        compiler_params=params,
        name="pack",
    )(key_in, value_in, filters)
    recv = lax.all_to_all(packed, "ctx", split_axis=0, concat_axis=0, tiled=True)
    own_skip = lax.dynamic_slice(skip, (lax.axis_index("ctx") * GROUP,), (GROUP,))
    summed = pl.pallas_call(
        conv_kernel,
        out_shape=jax.ShapeDtypeStruct((ctx, here, LANES), BF16),
        in_specs=[whole(), pl.BlockSpec(memory_space=pltpu.SMEM)],
        out_specs=whole(),
        scratch_shapes=[
            pltpu.VMEM((ctx * here, LANES), F32),
            pltpu.VMEM((ctx * here, LANES), F32),
            pltpu.VMEM((ctx * here, LANES), F32),
            pltpu.VMEM((PAD + LANES, LANES), F32),
            pltpu.VMEM((8 + LANES, LANES), F32),
            pltpu.VMEM((8 + LANES, LANES), F32),
            pltpu.VMEM((LANES, 2 * LANES), F32),
            pltpu.VMEM((8 * LANES, 2 * LANES), BF16),
            pltpu.VMEM((8 * LANES, 2 * LANES), BF16),
        ],
        compiler_params=params,
        name="conv",
    )(recv, own_skip)
    back = lax.all_to_all(summed, "ctx", split_axis=0, concat_axis=0, tiled=True)
    own = pl.pallas_call(
        energy_kernel,
        out_shape=jax.ShapeDtypeStruct((tp, blocks, LANES), F32),
        in_specs=[whole()],
        out_specs=whole(),
        compiler_params=params,
        name="energy",
    )(back)
    energy = lax.all_to_all(own, "tp", split_axis=0, concat_axis=0, tiled=True)
    return pl.pallas_call(
        functools.partial(finish_kernel, channels * tp),
        out_shape=jax.ShapeDtypeStruct((rows, channels), BF16),
        in_specs=[whole()] * 4,
        out_specs=whole(),
        compiler_params=params,
        name="finish",
    )(back, gate_in, energy, gain.reshape(1, channels))


def solution(mesh):
    in_specs = (P("ctx", "tp"), P("ctx", "tp"), P("ctx", "tp"), P("ctx", "tp"), P("tp"), P("tp"))
    out_specs = P("ctx", "tp")
    return jax.shard_map(
        per_device, mesh=mesh, in_specs=in_specs, out_specs=out_specs, check_vma=False
    )
```

```python
import functools

import jax
import jax.numpy as jnp
from jax import lax
from jax.experimental import pallas as pl
from jax.experimental.pallas import tpu as pltpu
from jax.sharding import PartitionSpec as P

EPSILON = 1e-05
LANES = 128
GROUP = 8
HOP = 32
STEP = 256
F32 = jnp.float32
BF16 = jnp.bfloat16


def whole():
    return pl.BlockSpec(memory_space=pltpu.VMEM)


def anywhere():
    return pl.BlockSpec(memory_space=pl.ANY)


def anywhere():
    return pl.BlockSpec(memory_space=pltpu.HBM)


def flip_blocks(rows):
    parts = []
    for a in range(rows.shape[0] // LANES):
        block = rows[a * LANES : (a + 1) * LANES, :].T
        parts.append(block.reshape(block.shape[0] // GROUP, GROUP, LANES))
    return jnp.concatenate(parts, axis=1)


def pack_kernel(
    place_ref, key_ref, value_ref, taps_ref, skip_ref, gain_ref, out_ref, rows_ref, key, value, taps, skip, in_sem
):
    half = out_ref.shape[1] // 2
    gain = rows_ref.at[GROUP:, :]
    loads = []
    pairs = ((taps_ref, taps), (key_ref, key), (value_ref, value), (skip_ref, skip), (gain_ref, gain))
    for i, (src, dst) in enumerate(pairs):
        load = pltpu.make_async_copy(src, dst, in_sem.at[i])
        load.start()
        loads.append(load)
    loads[0].wait()
    out_ref[:, half:, :] = flip_blocks(taps[...].astype(F32)).astype(BF16)
    loads[1].wait()
    loads[2].wait()
    mixed = key[...].astype(F32) * value[...].astype(F32)
    out_ref[:, :half, :] = flip_blocks(mixed).astype(BF16)
    loads[3].wait()
    loads[4].wait()
    for c in range(GROUP):
        rows_ref[c : c + 1, :] = jnp.full((1, LANES), skip[place_ref[0] * GROUP + c], F32)


def conv_kernel(
    recv_ref, rows_ref, out_ref, x_all, h_all, y_all, x_pad, h_pad, s_pad, acc, toe_0, toe_1, lhs_0, lhs_1
):
    owners, both, _ = recv_ref.shape
    half = both // 2
    x_all[...] = recv_ref[:, :half, :].astype(F32).reshape(owners * half, LANES)
    h_all[...] = recv_ref[:, half:, :].astype(F32).reshape(owners * half, LANES)
    x_pad[:8, :] = jnp.zeros((8, LANES), F32)
    h_pad[:8, :] = jnp.zeros((8, LANES), F32)
    s_pad[:, :8, :] = jnp.zeros((2, 8, LANES), F32)
    lane = lax.broadcasted_iota(jnp.int32, (8, LANES), 1)
    row = lax.broadcasted_iota(jnp.int32, (8, LANES), 0)
    edge = lane + row
    quarter = lax.broadcasted_iota(jnp.int32, (LANES, LANES), 1) // HOP
    toes = (toe_0, toe_1)
    sides = (lhs_0, lhs_1)

    def prepare(c):
        toe, side = toes[c % 2], sides[c % 2]
        h_pad[8:, :] = h_all[pl.ds(c, LANES, stride=GROUP), :]
        for k in range(LANES):
            now = jnp.broadcast_to(h_pad[8 + k : 9 + k, :], (8, LANES))
            before = jnp.broadcast_to(h_pad[7 + k : 8 + k, :], (8, LANES))
            tiles = []
            for v in range(0, HOP, 8):
                source = jnp.where(edge >= LANES - v, before, now)
                tiles.append(pltpu.roll(source, v, 1, stride=1, stride_axis=0))
            toe[k // 2 * HOP : (k // 2 + 1) * HOP, k % 2 * LANES : (k % 2 + 1) * LANES] = (
                jnp.concatenate(tiles, axis=0).astype(BF16)
            )
        x = x_all[pl.ds(c, LANES, stride=GROUP), :]
        x_pad[8:, :] = x
        late = [x] + [x_pad[8 - 2 * b : 8 - 2 * b + LANES, :] for b in (1, 2, 3)]
        turned = []
        for d in range(4):
            pick = late[d]
            for j in (1, 2, 3):
                pick = jnp.where(quarter == j, late[(j + d) % 4], pick)
            turned.append(pltpu.roll(pick, HOP * d, 1) if d else pick)
        for i in range(4):
            wide = turned[(-i) % 4]
            for b in (1, 2, 3):
                wide = jnp.where(quarter == b, turned[(b - i) % 4], wide)
            lower = jnp.concatenate([jnp.zeros((8, LANES), F32), wide[:-8]], axis=0)
            pair = jnp.concatenate([wide, lower], axis=1).astype(BF16)
            side[i, :, :STEP] = pair
            side[i, :, STEP:] = jnp.concatenate([jnp.zeros((16, STEP), BF16), pair[:-16]], axis=0)

    def convolve(c):
        toe, side = toes[c % 2], sides[c % 2]
        for g in range(0, 8, 2):
            live = LANES - 16 * g
            left = jnp.concatenate([side[i, :live, :] for i in range(4)], axis=0)
            part = jnp.dot(left, toe[STEP * g : STEP * (g + 2), :], preferred_element_type=F32)
            for i in range(4):
                if g == 0:
                    acc[i] = part[i * live : (i + 1) * live]
                else:
                    acc[i, 16 * g :, :] += part[i * live : (i + 1) * live]
        same, next_1, next_2 = acc[0, :, :LANES], acc[0, :, LANES:], jnp.zeros((LANES, LANES), F32)
        for i in range(1, 4):
            near = pltpu.roll(acc[i, :, :LANES], HOP * i, 1)
            far = pltpu.roll(acc[i, :, LANES:], HOP * i, 1)
            wrapped = quarter < i
            same = same + jnp.where(wrapped, 0.0, near)
            next_1 = next_1 + jnp.where(wrapped, near, far)
            next_2 = next_2 + jnp.where(wrapped, far, 0.0)
        s_pad[0, 8:, :] = next_1
        s_pad[1, 8:, :] = next_2
        x = x_all[pl.ds(c, LANES, stride=GROUP), :]
        conv = same + s_pad[0, 7 : 7 + LANES, :] + s_pad[1, 6 : 6 + LANES, :]
        y_all[pl.ds(c, LANES, stride=GROUP), :] = conv + rows_ref[c : c + 1, :] * x

    prepare(0)
    for c in range(GROUP):
        if c + 1 < GROUP:
            prepare(c + 1)
        convolve(c)
    out_ref[...] = y_all[...].reshape(out_ref.shape).astype(BF16)


def gate_kernel(back_ref, gate_ref, rows_ref, energy_ref, out_ref):
    owners, rows, _ = back_ref.shape
    blocks = rows // GROUP
    values = back_ref[...].astype(F32).reshape(owners, blocks, GROUP, LANES)
    own = jnp.sum(jnp.sum(values * values, axis=0), axis=1)
    for i in range(energy_ref.shape[0]):
        energy_ref[i] = own
    for a in range(blocks):
        block = values[:, a].reshape(owners * GROUP, LANES)
        span = slice(a * LANES, (a + 1) * LANES)
        for b in range(block.shape[0] // LANES):
            part = slice(b * LANES, (b + 1) * LANES)
            gain = rows_ref[GROUP + b : GROUP + b + 1, :]
            out_ref[span, part] = gate_ref[span, part].astype(F32) * block[part, :].T * gain


def scale_kernel(channels, gated_ref, energy_ref, out_ref, staged, sem):
    energy = jnp.sum(energy_ref[...], axis=0)
    scale = lax.rsqrt(energy / channels + EPSILON)
    stores = []
    for a in range(scale.shape[0]):
        column = jnp.broadcast_to(scale[a : a + 1, :], (LANES, LANES)).T
        span = slice(a * LANES, (a + 1) * LANES)
        for b in range(0, staged.shape[1], LANES):
            staged[span, b : b + LANES] = (gated_ref[span, b : b + LANES] * column).astype(BF16)
        store = pltpu.make_async_copy(staged.at[span, :], out_ref.at[span, :], sem.at[a])
        store.start()
        stores.append(store)
    for store in stores:
        store.wait()


def per_device(gate_in, key_in, value_in, filters, skip, gain):
    rows, channels = key_in.shape
    ctx = lax.axis_size("ctx")
    tp = lax.axis_size("tp")
    blocks = rows // LANES
    here = blocks * GROUP
    params = pltpu.CompilerParams(vmem_limit_bytes=32 * 1024 * 1024)
    packed, small = pl.pallas_call(
        pack_kernel,
        out_shape=[
            jax.ShapeDtypeStruct((ctx, 2 * here, LANES), BF16),
            jax.ShapeDtypeStruct((GROUP + channels // LANES, LANES), F32),
        ],
        in_specs=[pl.BlockSpec(memory_space=pltpu.SMEM)] + [anywhere()] * 5,
        out_specs=[whole()] * 2,
        scratch_shapes=[pltpu.VMEM((rows, channels), BF16)] * 3
        + [pltpu.SMEM((channels,), F32), pltpu.SemaphoreType.DMA((5,))],
        name="pack",
    )(lax.axis_index("ctx").reshape(1), key_in, value_in, filters, skip, gain.reshape(-1, LANES))
    recv = lax.all_to_all(packed, "ctx", split_axis=0, concat_axis=0, tiled=True)
    summed = pl.pallas_call(
        conv_kernel,
        out_shape=jax.ShapeDtypeStruct((ctx, here, LANES), BF16),
        in_specs=[whole()] * 2,
        out_specs=whole(),
        scratch_shapes=[pltpu.VMEM((ctx * here, LANES), F32)] * 3
        + [
            pltpu.VMEM((8 + LANES, LANES), F32),
            pltpu.VMEM((8 + LANES, LANES), F32),
            pltpu.VMEM((2, 8 + LANES, LANES), F32),
            pltpu.VMEM((4, LANES, STEP), F32),
            pltpu.VMEM((LANES // 2 * HOP, STEP), BF16),
            pltpu.VMEM((LANES // 2 * HOP, STEP), BF16),
            pltpu.VMEM((4, LANES, 2 * STEP), BF16),
            pltpu.VMEM((4, LANES, 2 * STEP), BF16),
        ],
        compiler_params=params,
        name="conv",
    )(recv, small)
    back = lax.all_to_all(summed, "ctx", split_axis=0, concat_axis=0, tiled=True)
    own, gated = pl.pallas_call(
        gate_kernel,
        out_shape=[
            jax.ShapeDtypeStruct((tp, blocks, LANES), F32),
            jax.ShapeDtypeStruct((rows, channels), F32),
        ],
        in_specs=[whole()] * 3,
        out_specs=[whole()] * 2,
        compiler_params=params,
        name="gate",
    )(back, gate_in, small)
    energy = lax.all_to_all(own, "tp", split_axis=0, concat_axis=0, tiled=True)
    return pl.pallas_call(
        functools.partial(scale_kernel, channels * tp),
        out_shape=jax.ShapeDtypeStruct((rows, channels), BF16),
        in_specs=[whole()] * 2,
        out_specs=anywhere(),
        scratch_shapes=[pltpu.VMEM((rows, channels), BF16), pltpu.SemaphoreType.DMA((blocks,))],
        compiler_params=params,
        name="scale",
    )(gated, energy)


def solution(mesh):
    in_specs = (P("ctx", "tp"), P("ctx", "tp"), P("ctx", "tp"), P("ctx", "tp"), P("tp"), P("tp"))
    out_specs = P("ctx", "tp")
    return jax.shard_map(
        per_device, mesh=mesh, in_specs=in_specs, out_specs=out_specs, check_vma=False
    )
```

```python
import functools

import jax
import jax.numpy as jnp
from jax import lax
from jax.experimental import pallas as pl
from jax.experimental.pallas import tpu as pltpu
from jax.sharding import PartitionSpec as P

EPSILON = 1e-05
LANES = 128
GROUP = 8
HOP = 32
STEP = 256
ROWS = 32
F32 = jnp.float32
BF16 = jnp.bfloat16


def whole():
    return pl.BlockSpec(memory_space=pltpu.VMEM)


def anywhere():
    return pl.BlockSpec(memory_space=pl.ANY)


def anywhere():
    return pl.BlockSpec(memory_space=pltpu.HBM)


def flip_blocks(rows):
    parts = []
    for a in range(rows.shape[0] // LANES):
        block = rows[a * LANES : (a + 1) * LANES, :].T
        parts.append(block.reshape(block.shape[0] // GROUP, GROUP, LANES))
    return jnp.concatenate(parts, axis=1)


def pack_kernel(
    place_ref, key_ref, value_ref, taps_ref, skip_ref, gain_ref, out_ref, rows_ref, key, value, taps, skip, in_sem
):
    half = out_ref.shape[1] // 2
    gain = rows_ref.at[GROUP:, :]
    loads = []
    pairs = ((taps_ref, taps), (key_ref, key), (value_ref, value), (skip_ref, skip), (gain_ref, gain))
    for i, (src, dst) in enumerate(pairs):
        load = pltpu.make_async_copy(src, dst, in_sem.at[i])
        load.start()
        loads.append(load)
    loads[0].wait()
    out_ref[:, half:, :] = flip_blocks(taps[...].astype(F32)).astype(BF16)
    loads[1].wait()
    loads[2].wait()
    mixed = key[...].astype(F32) * value[...].astype(F32)
    out_ref[:, :half, :] = flip_blocks(mixed).astype(BF16)
    loads[3].wait()
    loads[4].wait()
    for c in range(GROUP):
        rows_ref[c : c + 1, :] = jnp.full((1, LANES), skip[place_ref[0] * GROUP + c], F32)


def conv_kernel(
    recv_ref, rows_ref, out_ref, x_all, h_all, y_all, x_pad, h_pad, s_pad, toe_0, toe_1, side_0, side_1
):
    owners, both, _ = recv_ref.shape
    half = both // 2
    x_all[...] = recv_ref[:, :half, :].astype(F32).reshape(owners * half, LANES)
    h_all[...] = recv_ref[:, half:, :].astype(F32).reshape(owners * half, LANES)
    x_pad[:8, :] = jnp.zeros((8, LANES), F32)
    h_pad[:8, :] = jnp.zeros((8, LANES), F32)
    s_pad[:, :8, :] = jnp.zeros((2, 8, LANES), F32)
    toes = (toe_0, toe_1)
    sides = (side_0, side_1)
    for side in sides:
        side[:, :16, :] = jnp.zeros((4, 16, STEP), BF16)
    lane = lax.broadcasted_iota(jnp.int32, (8, LANES), 1)
    row = lax.broadcasted_iota(jnp.int32, (8, LANES), 0)
    edge = lane + row
    quarter = lax.broadcasted_iota(jnp.int32, (ROWS, LANES), 1) // HOP

    def fetch(c):
        h_pad[8:, :] = h_all[pl.ds(c, LANES, stride=GROUP), :]
        x_pad[8:, :] = x_all[pl.ds(c, LANES, stride=GROUP), :]

    def build_toe(c, s):
        toe = toes[c % 2]
        for k in range(ROWS * s, ROWS * (s + 1)):
            now = jnp.broadcast_to(h_pad[8 + k : 9 + k, :], (8, LANES))
            before = jnp.broadcast_to(h_pad[7 + k : 8 + k, :], (8, LANES))
            tiles = []
            for v in range(0, HOP, 8):
                source = jnp.where(edge >= LANES - v, before, now)
                tiles.append(pltpu.roll(source, v, 1, stride=1, stride_axis=0))
            toe[k // 2 * HOP : (k // 2 + 1) * HOP, k % 2 * LANES : (k % 2 + 1) * LANES] = (
                jnp.concatenate(tiles, axis=0).astype(BF16)
            )

    def build_side(c, s, above):
        side = sides[c % 2]
        low = ROWS * s
        late = [x_pad[8 - 2 * b + low : 8 - 2 * b + low + ROWS, :] for b in range(4)]
        turned = []
        for d in range(4):
            pick = late[d]
            for j in (1, 2, 3):
                pick = jnp.where(quarter == j, late[(j + d) % 4], pick)
            turned.append(pltpu.roll(pick, HOP * d, 1) if d else pick)
        last = []
        for j in range(4):
            wide = turned[(-j) % 4]
            for b in (1, 2, 3):
                wide = jnp.where(quarter == b, turned[(b - j) % 4], wide)
            lower = jnp.concatenate([above[j], wide[:-8]], axis=0)
            side[j, 16 + low : 16 + low + ROWS, :] = jnp.concatenate([wide, lower], axis=1).astype(BF16)
            last.append(wide[-8:])
        return last

    def product(c, s):
        toe, side = toes[c % 2], sides[c % 2]
        count = 2 * s + 2
        left = []
        for j in range(4):
            starts = [16 + ROWS * s - 16 * g for g in range(count)]
            left.append(jnp.concatenate([side[j, i : i + ROWS, :] for i in starts], axis=1))
        return jnp.dot(
            jnp.concatenate(left, axis=0), toe[: STEP * count, :], preferred_element_type=F32
        )

    def overlap_add(c, s, part):
        low = ROWS * s
        same, next_1 = part[:ROWS, :LANES], part[:ROWS, LANES:]
        next_2 = jnp.zeros((ROWS, LANES), F32)
        for j in range(1, 4):
            near = pltpu.roll(part[ROWS * j : ROWS * (j + 1), :LANES], HOP * j, 1)
            far = pltpu.roll(part[ROWS * j : ROWS * (j + 1), LANES:], HOP * j, 1)
            wrapped = quarter < j
            same = same + jnp.where(wrapped, 0.0, near)
            next_1 = next_1 + jnp.where(wrapped, near, far)
            next_2 = next_2 + jnp.where(wrapped, far, 0.0)
        s_pad[0, 8 + low : 8 + low + ROWS, :] = next_1
        s_pad[1, 8 + low : 8 + low + ROWS, :] = next_2
        conv = same + s_pad[0, 7 + low : 7 + low + ROWS, :] + s_pad[1, 6 + low : 6 + low + ROWS, :]
        own = pl.ds(GROUP * low + c, ROWS, stride=GROUP)
        y_all[own, :] = conv + rows_ref[c : c + 1, :] * x_all[own, :]

    steps = LANES // ROWS
    nothing = [jnp.zeros((8, LANES), F32)] * 4
    fetch(0)
    above = nothing
    for s in range(steps):
        above = build_side(0, s, above)
        build_toe(0, s)
    pending = None
    for c in range(GROUP):
        if c + 1 < GROUP:
            fetch(c + 1)
        above = nothing
        for s in range(steps):
            if c + 1 < GROUP:
                above = build_side(c + 1, s, above)
                build_toe(c + 1, s)
            if pending is not None:
                overlap_add(*pending)
            pending = (c, s, product(c, s))
    overlap_add(*pending)
    out_ref[...] = y_all[...].reshape(out_ref.shape).astype(BF16)


def gate_kernel(back_ref, gate_ref, rows_ref, energy_ref, out_ref):
    owners, rows, _ = back_ref.shape
    blocks = rows // GROUP
    values = back_ref[...].astype(F32).reshape(owners, blocks, GROUP, LANES)
    own = jnp.sum(jnp.sum(values * values, axis=0), axis=1)
    for i in range(energy_ref.shape[0]):
        energy_ref[i] = own
    for a in range(blocks):
        block = values[:, a].reshape(owners * GROUP, LANES)
        span = slice(a * LANES, (a + 1) * LANES)
        for b in range(block.shape[0] // LANES):
            part = slice(b * LANES, (b + 1) * LANES)
            gain = rows_ref[GROUP + b : GROUP + b + 1, :]
            out_ref[span, part] = gate_ref[span, part].astype(F32) * block[part, :].T * gain


def scale_kernel(channels, gated_ref, energy_ref, out_ref, staged, sem):
    energy = jnp.sum(energy_ref[...], axis=0)
    scale = lax.rsqrt(energy / channels + EPSILON)
    stores = []
    for a in range(scale.shape[0]):
        column = jnp.broadcast_to(scale[a : a + 1, :], (LANES, LANES)).T
        span = slice(a * LANES, (a + 1) * LANES)
        for b in range(0, staged.shape[1], LANES):
            staged[span, b : b + LANES] = (gated_ref[span, b : b + LANES] * column).astype(BF16)
        store = pltpu.make_async_copy(staged.at[span, :], out_ref.at[span, :], sem.at[a])
        store.start()
        stores.append(store)
    for store in stores:
        store.wait()


def per_device(gate_in, key_in, value_in, filters, skip, gain):
    rows, channels = key_in.shape
    ctx = lax.axis_size("ctx")
    tp = lax.axis_size("tp")
    blocks = rows // LANES
    here = blocks * GROUP
    params = pltpu.CompilerParams(vmem_limit_bytes=32 * 1024 * 1024)
    packed, small = pl.pallas_call(
        pack_kernel,
        out_shape=[
            jax.ShapeDtypeStruct((ctx, 2 * here, LANES), BF16),
            jax.ShapeDtypeStruct((GROUP + channels // LANES, LANES), F32),
        ],
        in_specs=[pl.BlockSpec(memory_space=pltpu.SMEM)] + [anywhere()] * 5,
        out_specs=[whole()] * 2,
        scratch_shapes=[pltpu.VMEM((rows, channels), BF16)] * 3
        + [pltpu.SMEM((channels,), F32), pltpu.SemaphoreType.DMA((5,))],
        compiler_params=params,
        name="pack",
    )(
        lax.axis_index("ctx").reshape(1),
        *(pltpu.with_memory_space_constraint(v, pltpu.HBM) for v in (key_in, value_in, filters, skip)),
        pltpu.with_memory_space_constraint(gain.reshape(-1, LANES), pltpu.HBM),
    )
    recv = lax.all_to_all(packed, "ctx", split_axis=0, concat_axis=0, tiled=True)
    summed = pl.pallas_call(
        conv_kernel,
        out_shape=jax.ShapeDtypeStruct((ctx, here, LANES), BF16),
        in_specs=[whole()] * 2,
        out_specs=whole(),
        scratch_shapes=[pltpu.VMEM((ctx * here, LANES), F32)] * 3
        + [
            pltpu.VMEM((8 + LANES, LANES), F32),
            pltpu.VMEM((8 + LANES, LANES), F32),
            pltpu.VMEM((2, 8 + LANES, LANES), F32),
            pltpu.VMEM((LANES // 2 * HOP, STEP), BF16),
            pltpu.VMEM((LANES // 2 * HOP, STEP), BF16),
            pltpu.VMEM((4, 16 + LANES, STEP), BF16),
            pltpu.VMEM((4, 16 + LANES, STEP), BF16),
        ],
        compiler_params=params,
        name="conv",
    )(recv, small)
    back = lax.all_to_all(summed, "ctx", split_axis=0, concat_axis=0, tiled=True)
    own, gated = pl.pallas_call(
        gate_kernel,
        out_shape=[
            jax.ShapeDtypeStruct((tp, blocks, LANES), F32),
            jax.ShapeDtypeStruct((rows, channels), F32),
        ],
        in_specs=[whole()] * 3,
        out_specs=[whole()] * 2,
        compiler_params=params,
        name="gate",
    )(back, gate_in, small)
    energy = lax.all_to_all(own, "tp", split_axis=0, concat_axis=0, tiled=True)
    return pl.pallas_call(
        functools.partial(scale_kernel, channels * tp),
        out_shape=jax.ShapeDtypeStruct((rows, channels), BF16),
        in_specs=[whole()] * 2,
        out_specs=anywhere(),
        scratch_shapes=[pltpu.VMEM((rows, channels), BF16), pltpu.SemaphoreType.DMA((blocks,))],
        compiler_params=params,
        name="scale",
    )(gated, energy)


def solution(mesh):
    in_specs = (P("ctx", "tp"), P("ctx", "tp"), P("ctx", "tp"), P("ctx", "tp"), P("tp"), P("tp"))
    out_specs = P("ctx", "tp")
    return jax.shard_map(
        per_device, mesh=mesh, in_specs=in_specs, out_specs=out_specs, check_vma=False
    )
```

```python
import functools

import jax
import jax.numpy as jnp
from jax import lax
from jax.experimental import pallas as pl
from jax.experimental.pallas import tpu as pltpu
from jax.sharding import PartitionSpec as P

EPSILON = 1e-05
LANES = 128
GROUP = 8
HOP = 32
STEP = 256
ROWS = 32
F32 = jnp.float32
BF16 = jnp.bfloat16


def whole():
    return pl.BlockSpec(memory_space=pltpu.VMEM)


def anywhere():
    return pl.BlockSpec(memory_space=pl.ANY)


def anywhere():
    return pl.BlockSpec(memory_space=pltpu.HBM)


def flip_blocks(rows):
    parts = []
    for a in range(rows.shape[0] // LANES):
        block = rows[a * LANES : (a + 1) * LANES, :].T
        parts.append(block.reshape(block.shape[0] // GROUP, GROUP, LANES))
    return jnp.concatenate(parts, axis=1)


def pack_kernel(
    place_ref, key_ref, value_ref, taps_ref, skip_ref, gain_ref, out_ref, rows_ref, key, value, taps, skip, in_sem
):
    half = out_ref.shape[1] // 2
    gain = rows_ref.at[GROUP:, :]
    loads = []
    pairs = ((taps_ref, taps), (key_ref, key), (value_ref, value), (skip_ref, skip), (gain_ref, gain))
    for i, (src, dst) in enumerate(pairs):
        load = pltpu.make_async_copy(src, dst, in_sem.at[i])
        load.start()
        loads.append(load)
    loads[0].wait()
    out_ref[:, half:, :] = flip_blocks(taps[...].astype(F32)).astype(BF16)
    loads[1].wait()
    loads[2].wait()
    mixed = key[...].astype(F32) * value[...].astype(F32)
    out_ref[:, :half, :] = flip_blocks(mixed).astype(BF16)
    loads[3].wait()
    loads[4].wait()
    for c in range(GROUP):
        rows_ref[c : c + 1, :] = jnp.full((1, LANES), skip[place_ref[0] * GROUP + c], F32)


def conv_kernel(
    recv_ref, rows_ref, out_ref, x_all, h_all, y_all, x_pad, h_pad, s_pad, far_pad, toe_0, toe_1, side_0, side_1
):
    owners, both, _ = recv_ref.shape
    half = both // 2
    x_all[...] = recv_ref[:, :half, :].astype(F32).reshape(owners * half, LANES)
    h_all[...] = recv_ref[:, half:, :].astype(F32).reshape(owners * half, LANES)
    x_pad[:8, :] = jnp.zeros((8, LANES), F32)
    h_pad[:8, :] = jnp.zeros((8, LANES), F32)
    s_pad[:8, :] = jnp.zeros((8, LANES), F32)
    far_pad[:, :8, :] = jnp.zeros((4, 8, LANES), F32)
    toes = (toe_0, toe_1)
    sides = (side_0, side_1)
    for side in sides:
        side[:, :16, :] = jnp.zeros((4, 16, STEP), BF16)
    lane = lax.broadcasted_iota(jnp.int32, (8, LANES), 1)
    row = lax.broadcasted_iota(jnp.int32, (8, LANES), 0)
    edge = lane + row
    quarter = lax.broadcasted_iota(jnp.int32, (ROWS, LANES), 1) // HOP

    def fetch(c):
        h_pad[8:, :] = h_all[pl.ds(c, LANES, stride=GROUP), :]
        x_pad[8:, :] = x_all[pl.ds(c, LANES, stride=GROUP), :]

    def build_toe(c, s):
        toe = toes[c % 2]
        for k in range(ROWS * s, ROWS * (s + 1)):
            now = jnp.broadcast_to(h_pad[8 + k : 9 + k, :], (8, LANES))
            before = jnp.broadcast_to(h_pad[7 + k : 8 + k, :], (8, LANES))
            tiles = []
            for v in range(0, HOP, 8):
                source = jnp.where(edge >= LANES - v, before, now)
                tiles.append(pltpu.roll(source, v, 1, stride=1, stride_axis=0))
            toe[k // 2 * HOP : (k // 2 + 1) * HOP, k % 2 * LANES : (k % 2 + 1) * LANES] = (
                jnp.concatenate(tiles, axis=0).astype(BF16)
            )

    def build_side(c, s, above):
        side = sides[c % 2]
        low = ROWS * s
        late = [x_pad[8 - 2 * b + low : 8 - 2 * b + low + ROWS, :] for b in range(4)]
        turned = []
        for d in range(4):
            pick = late[d]
            for j in (1, 2, 3):
                pick = jnp.where(quarter == j, late[(j + d) % 4], pick)
            turned.append(pltpu.roll(pick, HOP * d, 1) if d else pick)
        last = []
        for j in range(4):
            wide = turned[(-j) % 4]
            for b in (1, 2, 3):
                wide = jnp.where(quarter == b, turned[(b - j) % 4], wide)
            lower = jnp.concatenate([above[j], wide[:-8]], axis=0)
            side[j, 16 + low : 16 + low + ROWS, :] = jnp.concatenate([wide, lower], axis=1).astype(BF16)
            last.append(wide[-8:])
        return last

    def product(c, s):
        toe, side = toes[c % 2], sides[c % 2]
        count = 2 * s + 2
        left = []
        for j in range(4):
            starts = [16 + ROWS * s - 16 * g for g in range(count)]
            left.append(jnp.concatenate([side[j, i : i + ROWS, :] for i in starts], axis=1))
        return jnp.dot(
            jnp.concatenate(left, axis=0), toe[: STEP * count, :], preferred_element_type=F32
        )

    def overlap_add(c, s, part):
        low = ROWS * s
        late = slice(7 + low, 7 + low + ROWS)
        same, carried = None, jnp.zeros((ROWS, LANES), F32)
        for j in range(4):
            span = slice(ROWS * j, ROWS * (j + 1))
            far_pad[j, 8 + low : 8 + low + ROWS, :] = part[span, LANES:]
            total = part[span, :LANES] + far_pad[j, late, :]
            if j == 0:
                same = total
                continue
            total = pltpu.roll(total, HOP * j, 1)
            wrapped = quarter < j
            same = same + jnp.where(wrapped, 0.0, total)
            carried = carried + jnp.where(wrapped, total, 0.0)
        s_pad[8 + low : 8 + low + ROWS, :] = carried
        own = pl.ds(GROUP * low + c, ROWS, stride=GROUP)
        y_all[own, :] = same + s_pad[late, :] + rows_ref[c : c + 1, :] * x_all[own, :]

    steps = LANES // ROWS
    nothing = [jnp.zeros((8, LANES), F32)] * 4
    fetch(0)
    above = nothing
    for s in range(steps):
        above = build_side(0, s, above)
        build_toe(0, s)
    pending = None
    for c in range(GROUP):
        if c + 1 < GROUP:
            fetch(c + 1)
        above = nothing
        for s in range(steps):
            if c + 1 < GROUP:
                above = build_side(c + 1, s, above)
                build_toe(c + 1, s)
            if pending is not None:
                overlap_add(*pending)
            pending = (c, s, product(c, s))
    overlap_add(*pending)
    out_ref[...] = y_all[...].reshape(out_ref.shape).astype(BF16)


def gate_kernel(back_ref, gate_ref, rows_ref, energy_ref, out_ref):
    owners, rows, _ = back_ref.shape
    blocks = rows // GROUP
    values = back_ref[...].astype(F32).reshape(owners, blocks, GROUP, LANES)
    own = jnp.sum(jnp.sum(values * values, axis=0), axis=1)
    for i in range(energy_ref.shape[0]):
        energy_ref[i] = own
    for a in range(blocks):
        block = values[:, a].reshape(owners * GROUP, LANES)
        span = slice(a * LANES, (a + 1) * LANES)
        for b in range(block.shape[0] // LANES):
            part = slice(b * LANES, (b + 1) * LANES)
            gain = rows_ref[GROUP + b : GROUP + b + 1, :]
            out_ref[span, part] = gate_ref[span, part].astype(F32) * block[part, :].T * gain


def scale_kernel(channels, gated_ref, energy_ref, out_ref, staged, sem):
    energy = jnp.sum(energy_ref[...], axis=0)
    scale = lax.rsqrt(energy / channels + EPSILON)
    stores = []
    for a in range(scale.shape[0]):
        column = jnp.broadcast_to(scale[a : a + 1, :], (LANES, LANES)).T
        span = slice(a * LANES, (a + 1) * LANES)
        for b in range(0, staged.shape[1], LANES):
            staged[span, b : b + LANES] = (gated_ref[span, b : b + LANES] * column).astype(BF16)
        store = pltpu.make_async_copy(staged.at[span, :], out_ref.at[span, :], sem.at[a])
        store.start()
        stores.append(store)
    for store in stores:
        store.wait()


def per_device(gate_in, key_in, value_in, filters, skip, gain):
    rows, channels = key_in.shape
    ctx = lax.axis_size("ctx")
    tp = lax.axis_size("tp")
    blocks = rows // LANES
    here = blocks * GROUP
    params = pltpu.CompilerParams(vmem_limit_bytes=32 * 1024 * 1024)
    packed, small = pl.pallas_call(
        pack_kernel,
        out_shape=[
            jax.ShapeDtypeStruct((ctx, 2 * here, LANES), BF16),
            jax.ShapeDtypeStruct((GROUP + channels // LANES, LANES), F32),
        ],
        in_specs=[pl.BlockSpec(memory_space=pltpu.SMEM)] + [anywhere()] * 5,
        out_specs=[whole()] * 2,
        scratch_shapes=[pltpu.VMEM((rows, channels), BF16)] * 3
        + [pltpu.SMEM((channels,), F32), pltpu.SemaphoreType.DMA((5,))],
        compiler_params=params,
        name="pack",
    )(
        lax.axis_index("ctx").reshape(1),
        *(pltpu.with_memory_space_constraint(v, pltpu.HBM) for v in (key_in, value_in, filters, skip)),
        pltpu.with_memory_space_constraint(gain.reshape(-1, LANES), pltpu.HBM),
    )
    recv = lax.all_to_all(packed, "ctx", split_axis=0, concat_axis=0, tiled=True)
    summed = pl.pallas_call(
        conv_kernel,
        out_shape=jax.ShapeDtypeStruct((ctx, here, LANES), BF16),
        in_specs=[whole()] * 2,
        out_specs=whole(),
        scratch_shapes=[pltpu.VMEM((ctx * here, LANES), F32)] * 3
        + [
            pltpu.VMEM((8 + LANES, LANES), F32),
            pltpu.VMEM((8 + LANES, LANES), F32),
            pltpu.VMEM((8 + LANES, LANES), F32),
            pltpu.VMEM((4, 8 + LANES, LANES), F32),
            pltpu.VMEM((LANES // 2 * HOP, STEP), BF16),
            pltpu.VMEM((LANES // 2 * HOP, STEP), BF16),
            pltpu.VMEM((4, 16 + LANES, STEP), BF16),
            pltpu.VMEM((4, 16 + LANES, STEP), BF16),
        ],
        compiler_params=params,
        name="conv",
    )(recv, small)
    back = lax.all_to_all(summed, "ctx", split_axis=0, concat_axis=0, tiled=True)
    own, gated = pl.pallas_call(
        gate_kernel,
        out_shape=[
            jax.ShapeDtypeStruct((tp, blocks, LANES), F32),
            jax.ShapeDtypeStruct((rows, channels), F32),
        ],
        in_specs=[whole()] * 3,
        out_specs=[whole()] * 2,
        compiler_params=params,
        name="gate",
    )(back, gate_in, small)
    energy = lax.all_to_all(own, "tp", split_axis=0, concat_axis=0, tiled=True)
    return pl.pallas_call(
        functools.partial(scale_kernel, channels * tp),
        out_shape=jax.ShapeDtypeStruct((rows, channels), BF16),
        in_specs=[whole()] * 2,
        out_specs=anywhere(),
        scratch_shapes=[pltpu.VMEM((rows, channels), BF16), pltpu.SemaphoreType.DMA((blocks,))],
        compiler_params=params,
        name="scale",
    )(gated, energy)


def solution(mesh):
    in_specs = (P("ctx", "tp"), P("ctx", "tp"), P("ctx", "tp"), P("ctx", "tp"), P("tp"), P("tp"))
    out_specs = P("ctx", "tp")
    return jax.shard_map(
        per_device, mesh=mesh, in_specs=in_specs, out_specs=out_specs, check_vma=False
    )
```

```python
import functools

import jax
import jax.numpy as jnp
from jax import lax
from jax.experimental import pallas as pl
from jax.experimental.pallas import tpu as pltpu
from jax.sharding import PartitionSpec as P

EPSILON = 1e-05
LANES = 128
GROUP = 8
HOP = 32
STEP = 256
ROWS = 32
SEND_ORDER = [8 * x + (2 * x + y) % 8 for y in range(8) for x in range(4)]
RETURN_ORDER = [8 * x + y for y in (0, 4, 1, 5, 2, 6, 3, 7) for x in (0, 2, 1, 3)]
F32 = jnp.float32
BF16 = jnp.bfloat16


def whole():
    return pl.BlockSpec(memory_space=pltpu.VMEM)


def anywhere():
    return pl.BlockSpec(memory_space=pl.ANY)


def anywhere():
    return pl.BlockSpec(memory_space=pltpu.HBM)


def flip_blocks(rows):
    parts = []
    for a in range(rows.shape[0] // LANES):
        block = rows[a * LANES : (a + 1) * LANES, :].T
        parts.append(block.reshape(block.shape[0] // GROUP, GROUP, LANES))
    owners = jnp.concatenate(parts, axis=1)
    return jnp.stack([owners[d] for d in SEND_ORDER])


def pack_kernel(
    place_ref, key_ref, value_ref, taps_ref, skip_ref, gain_ref, out_ref, rows_ref, key, value, taps, skip, in_sem
):
    half = out_ref.shape[1] // 2
    gain = rows_ref.at[GROUP:, :]
    loads = []
    pairs = ((taps_ref, taps), (key_ref, key), (value_ref, value), (skip_ref, skip), (gain_ref, gain))
    for i, (src, dst) in enumerate(pairs):
        load = pltpu.make_async_copy(src, dst, in_sem.at[i])
        load.start()
        loads.append(load)
    loads[0].wait()
    out_ref[:, half:, :] = flip_blocks(taps[...].astype(F32)).astype(BF16)
    loads[1].wait()
    loads[2].wait()
    mixed = key[...].astype(F32) * value[...].astype(F32)
    out_ref[:, :half, :] = flip_blocks(mixed).astype(BF16)
    loads[3].wait()
    loads[4].wait()
    for c in range(GROUP):
        rows_ref[c : c + 1, :] = jnp.full((1, LANES), skip[place_ref[0] * GROUP + c], F32)


def conv_kernel(
    recv_ref, rows_ref, out_ref, x_all, h_all, y_all, x_pad, h_pad, s_pad, far_pad, toe_0, toe_1, side_0, side_1
):
    owners, both, _ = recv_ref.shape
    half = both // 2
    for i, d in enumerate(SEND_ORDER):
        x_all[d * half : (d + 1) * half, :] = recv_ref[i, :half, :].astype(F32)
        h_all[d * half : (d + 1) * half, :] = recv_ref[i, half:, :].astype(F32)
    x_pad[:8, :] = jnp.zeros((8, LANES), F32)
    h_pad[:8, :] = jnp.zeros((8, LANES), F32)
    s_pad[:8, :] = jnp.zeros((8, LANES), F32)
    far_pad[:, :8, :] = jnp.zeros((4, 8, LANES), F32)
    toes = (toe_0, toe_1)
    sides = (side_0, side_1)
    for side in sides:
        side[:, :16, :] = jnp.zeros((4, 16, STEP), BF16)
    lane = lax.broadcasted_iota(jnp.int32, (8, LANES), 1)
    row = lax.broadcasted_iota(jnp.int32, (8, LANES), 0)
    edge = lane + row
    quarter = lax.broadcasted_iota(jnp.int32, (ROWS, LANES), 1) // HOP

    def fetch(c):
        h_pad[8:, :] = h_all[pl.ds(c, LANES, stride=GROUP), :]
        x_pad[8:, :] = x_all[pl.ds(c, LANES, stride=GROUP), :]

    def build_toe(c, s):
        toe = toes[c % 2]
        for k in range(ROWS * s, ROWS * (s + 1)):
            now = jnp.broadcast_to(h_pad[8 + k : 9 + k, :], (8, LANES))
            before = jnp.broadcast_to(h_pad[7 + k : 8 + k, :], (8, LANES))
            tiles = []
            for v in range(0, HOP, 8):
                source = jnp.where(edge >= LANES - v, before, now)
                tiles.append(pltpu.roll(source, v, 1, stride=1, stride_axis=0))
            toe[k // 2 * HOP : (k // 2 + 1) * HOP, k % 2 * LANES : (k % 2 + 1) * LANES] = (
                jnp.concatenate(tiles, axis=0).astype(BF16)
            )

    def build_side(c, s, above):
        side = sides[c % 2]
        low = ROWS * s
        late = [x_pad[8 - 2 * b + low : 8 - 2 * b + low + ROWS, :] for b in range(4)]
        turned = []
        for d in range(4):
            pick = late[d]
            for j in (1, 2, 3):
                pick = jnp.where(quarter == j, late[(j + d) % 4], pick)
            turned.append(pltpu.roll(pick, HOP * d, 1) if d else pick)
        last = []
        for j in range(4):
            wide = turned[(-j) % 4]
            for b in (1, 2, 3):
                wide = jnp.where(quarter == b, turned[(b - j) % 4], wide)
            lower = jnp.concatenate([above[j], wide[:-8]], axis=0)
            side[j, 16 + low : 16 + low + ROWS, :] = jnp.concatenate([wide, lower], axis=1).astype(BF16)
            last.append(wide[-8:])
        return last

    def product(c, s):
        toe, side = toes[c % 2], sides[c % 2]
        count = 2 * s + 2
        left = []
        for j in range(4):
            starts = [16 + ROWS * s - 16 * g for g in range(count)]
            left.append(jnp.concatenate([side[j, i : i + ROWS, :] for i in starts], axis=1))
        return jnp.dot(
            jnp.concatenate(left, axis=0), toe[: STEP * count, :], preferred_element_type=F32
        )

    def overlap_add(c, s, part):
        low = ROWS * s
        late = slice(7 + low, 7 + low + ROWS)
        same, carried = None, jnp.zeros((ROWS, LANES), F32)
        for j in range(4):
            span = slice(ROWS * j, ROWS * (j + 1))
            far_pad[j, 8 + low : 8 + low + ROWS, :] = part[span, LANES:]
            total = part[span, :LANES] + far_pad[j, late, :]
            if j == 0:
                same = total
                continue
            total = pltpu.roll(total, HOP * j, 1)
            wrapped = quarter < j
            same = same + jnp.where(wrapped, 0.0, total)
            carried = carried + jnp.where(wrapped, total, 0.0)
        s_pad[8 + low : 8 + low + ROWS, :] = carried
        own = pl.ds(GROUP * low + c, ROWS, stride=GROUP)
        y_all[own, :] = same + s_pad[late, :] + rows_ref[c : c + 1, :] * x_all[own, :]

    steps = LANES // ROWS
    nothing = [jnp.zeros((8, LANES), F32)] * 4
    fetch(0)
    above = nothing
    for s in range(steps):
        above = build_side(0, s, above)
        build_toe(0, s)
    pending = None
    for c in range(GROUP):
        if c + 1 < GROUP:
            fetch(c + 1)
        above = nothing
        for s in range(steps):
            if c + 1 < GROUP:
                above = build_side(c + 1, s, above)
                build_toe(c + 1, s)
            if pending is not None:
                overlap_add(*pending)
            pending = (c, s, product(c, s))
    overlap_add(*pending)
    summed = y_all[...].reshape(out_ref.shape)
    out_ref[...] = jnp.stack([summed[d] for d in RETURN_ORDER]).astype(BF16)


def gate_kernel(back_ref, gate_ref, rows_ref, energy_ref, out_ref):
    owners, rows, _ = back_ref.shape
    blocks = rows // GROUP
    values = back_ref[...].astype(F32)
    values = jnp.stack([values[RETURN_ORDER.index(d)] for d in range(owners)])
    values = values.reshape(owners, blocks, GROUP, LANES)
    own = jnp.sum(jnp.sum(values * values, axis=0), axis=1)
    for i in range(energy_ref.shape[0]):
        energy_ref[i] = own
    for a in range(blocks):
        block = values[:, a].reshape(owners * GROUP, LANES)
        span = slice(a * LANES, (a + 1) * LANES)
        for b in range(block.shape[0] // LANES):
            part = slice(b * LANES, (b + 1) * LANES)
            gain = rows_ref[GROUP + b : GROUP + b + 1, :]
            out_ref[span, part] = gate_ref[span, part].astype(F32) * block[part, :].T * gain


def scale_kernel(channels, gated_ref, energy_ref, out_ref, staged, sem):
    energy = jnp.sum(energy_ref[...], axis=0)
    scale = lax.rsqrt(energy / channels + EPSILON)
    stores = []
    for a in range(scale.shape[0]):
        column = jnp.broadcast_to(scale[a : a + 1, :], (LANES, LANES)).T
        span = slice(a * LANES, (a + 1) * LANES)
        for b in range(0, staged.shape[1], LANES):
            staged[span, b : b + LANES] = (gated_ref[span, b : b + LANES] * column).astype(BF16)
        store = pltpu.make_async_copy(staged.at[span, :], out_ref.at[span, :], sem.at[a])
        store.start()
        stores.append(store)
    for store in stores:
        store.wait()


def per_device(gate_in, key_in, value_in, filters, skip, gain):
    rows, channels = key_in.shape
    ctx = lax.axis_size("ctx")
    tp = lax.axis_size("tp")
    blocks = rows // LANES
    here = blocks * GROUP
    params = pltpu.CompilerParams(vmem_limit_bytes=32 * 1024 * 1024)
    packed, small = pl.pallas_call(
        pack_kernel,
        out_shape=[
            jax.ShapeDtypeStruct((ctx, 2 * here, LANES), BF16),
            jax.ShapeDtypeStruct((GROUP + channels // LANES, LANES), F32),
        ],
        in_specs=[pl.BlockSpec(memory_space=pltpu.SMEM)] + [anywhere()] * 5,
        out_specs=[whole()] * 2,
        scratch_shapes=[pltpu.VMEM((rows, channels), BF16)] * 3
        + [pltpu.SMEM((channels,), F32), pltpu.SemaphoreType.DMA((5,))],
        compiler_params=params,
        name="pack",
    )(
        lax.axis_index("ctx").reshape(1),
        *(pltpu.with_memory_space_constraint(v, pltpu.HBM) for v in (key_in, value_in, filters, skip)),
        pltpu.with_memory_space_constraint(gain.reshape(-1, LANES), pltpu.HBM),
    )
    recv = lax.all_to_all(
        packed, "ctx", split_axis=0, concat_axis=0, tiled=True, axis_index_groups=[SEND_ORDER]
    )
    summed = pl.pallas_call(
        conv_kernel,
        out_shape=jax.ShapeDtypeStruct((ctx, here, LANES), BF16),
        in_specs=[whole()] * 2,
        out_specs=whole(),
        scratch_shapes=[pltpu.VMEM((ctx * here, LANES), F32)] * 3
        + [
            pltpu.VMEM((8 + LANES, LANES), F32),
            pltpu.VMEM((8 + LANES, LANES), F32),
            pltpu.VMEM((8 + LANES, LANES), F32),
            pltpu.VMEM((4, 8 + LANES, LANES), F32),
            pltpu.VMEM((LANES // 2 * HOP, STEP), BF16),
            pltpu.VMEM((LANES // 2 * HOP, STEP), BF16),
            pltpu.VMEM((4, 16 + LANES, STEP), BF16),
            pltpu.VMEM((4, 16 + LANES, STEP), BF16),
        ],
        compiler_params=params,
        name="conv",
    )(recv, small)
    back = lax.all_to_all(
        summed, "ctx", split_axis=0, concat_axis=0, tiled=True, axis_index_groups=[RETURN_ORDER]
    )
    own, gated = pl.pallas_call(
        gate_kernel,
        out_shape=[
            jax.ShapeDtypeStruct((tp, blocks, LANES), F32),
            jax.ShapeDtypeStruct((rows, channels), F32),
        ],
        in_specs=[whole()] * 3,
        out_specs=[whole()] * 2,
        compiler_params=params,
        name="gate",
    )(back, gate_in, small)
    energy = lax.all_to_all(own, "tp", split_axis=0, concat_axis=0, tiled=True)
    return pl.pallas_call(
        functools.partial(scale_kernel, channels * tp),
        out_shape=jax.ShapeDtypeStruct((rows, channels), BF16),
        in_specs=[whole()] * 2,
        out_specs=anywhere(),
        scratch_shapes=[pltpu.VMEM((rows, channels), BF16), pltpu.SemaphoreType.DMA((blocks,))],
        compiler_params=params,
        name="scale",
    )(gated, energy)


def solution(mesh):
    in_specs = (P("ctx", "tp"), P("ctx", "tp"), P("ctx", "tp"), P("ctx", "tp"), P("tp"), P("tp"))
    out_specs = P("ctx", "tp")
    return jax.shard_map(
        per_device, mesh=mesh, in_specs=in_specs, out_specs=out_specs, check_vma=False
    )
```

```python
import functools

import jax
import jax.numpy as jnp
from jax import lax
from jax.experimental import pallas as pl
from jax.experimental.pallas import tpu as pltpu
from jax.sharding import PartitionSpec as P

EPSILON = 1e-05
LANES = 128
GROUP = 8
HOP = 32
STEP = 256
ROWS = 32
SEND_ORDER = [8 * x + (2 * x + y) % 8 for y in range(8) for x in range(4)]
RETURN_ORDER = [int(format(i, "05b")[::-1], 2) for i in range(32)]
F32 = jnp.float32
BF16 = jnp.bfloat16


def whole():
    return pl.BlockSpec(memory_space=pltpu.VMEM)


def anywhere():
    return pl.BlockSpec(memory_space=pl.ANY)


def anywhere():
    return pl.BlockSpec(memory_space=pltpu.HBM)


def flip_blocks(rows):
    parts = []
    for a in range(rows.shape[0] // LANES):
        block = rows[a * LANES : (a + 1) * LANES, :].T
        parts.append(block.reshape(block.shape[0] // GROUP, GROUP, LANES))
    owners = jnp.concatenate(parts, axis=1)
    return jnp.stack([owners[d] for d in SEND_ORDER])


def pack_kernel(
    place_ref, key_ref, value_ref, taps_ref, skip_ref, gain_ref, out_ref, rows_ref, key, value, taps, skip, in_sem
):
    half = out_ref.shape[1] // 2
    gain = rows_ref.at[GROUP:, :]
    loads = []
    pairs = ((taps_ref, taps), (key_ref, key), (value_ref, value), (skip_ref, skip), (gain_ref, gain))
    for i, (src, dst) in enumerate(pairs):
        load = pltpu.make_async_copy(src, dst, in_sem.at[i])
        load.start()
        loads.append(load)
    loads[0].wait()
    out_ref[:, half:, :] = flip_blocks(taps[...].astype(F32)).astype(BF16)
    loads[1].wait()
    loads[2].wait()
    mixed = key[...].astype(F32) * value[...].astype(F32)
    out_ref[:, :half, :] = flip_blocks(mixed).astype(BF16)
    loads[3].wait()
    loads[4].wait()
    for c in range(GROUP):
        rows_ref[c : c + 1, :] = jnp.full((1, LANES), skip[place_ref[0] * GROUP + c], F32)


def conv_kernel(
    recv_ref, rows_ref, out_ref, x_all, h_all, y_all, x_pad, h_pad, s_pad, far_pad, toe_0, toe_1, side_0, side_1
):
    owners, both, _ = recv_ref.shape
    half = both // 2
    for i, d in enumerate(SEND_ORDER):
        x_all[d * half : (d + 1) * half, :] = recv_ref[i, :half, :].astype(F32)
        h_all[d * half : (d + 1) * half, :] = recv_ref[i, half:, :].astype(F32)
    x_pad[:8, :] = jnp.zeros((8, LANES), F32)
    h_pad[:8, :] = jnp.zeros((8, LANES), F32)
    s_pad[:8, :] = jnp.zeros((8, LANES), F32)
    far_pad[:, :8, :] = jnp.zeros((4, 8, LANES), F32)
    toes = (toe_0, toe_1)
    sides = (side_0, side_1)
    for side in sides:
        side[:, :16, :] = jnp.zeros((4, 16, STEP), BF16)
    lane = lax.broadcasted_iota(jnp.int32, (8, LANES), 1)
    row = lax.broadcasted_iota(jnp.int32, (8, LANES), 0)
    edge = lane + row
    quarter = lax.broadcasted_iota(jnp.int32, (ROWS, LANES), 1) // HOP

    def fetch(c):
        h_pad[8:, :] = h_all[pl.ds(c, LANES, stride=GROUP), :]
        x_pad[8:, :] = x_all[pl.ds(c, LANES, stride=GROUP), :]

    def build_toe(c, s):
        toe = toes[c % 2]
        for k in range(ROWS * s, ROWS * (s + 1)):
            now = jnp.broadcast_to(h_pad[8 + k : 9 + k, :], (8, LANES))
            before = jnp.broadcast_to(h_pad[7 + k : 8 + k, :], (8, LANES))
            tiles = []
            for v in range(0, HOP, 8):
                source = jnp.where(edge >= LANES - v, before, now)
                tiles.append(pltpu.roll(source, v, 1, stride=1, stride_axis=0))
            toe[k // 2 * HOP : (k // 2 + 1) * HOP, k % 2 * LANES : (k % 2 + 1) * LANES] = (
                jnp.concatenate(tiles, axis=0).astype(BF16)
            )

    def build_side(c, s, above):
        side = sides[c % 2]
        low = ROWS * s
        late = [x_pad[8 - 2 * b + low : 8 - 2 * b + low + ROWS, :] for b in range(4)]
        turned = []
        for d in range(4):
            pick = late[d]
            for j in (1, 2, 3):
                pick = jnp.where(quarter == j, late[(j + d) % 4], pick)
            turned.append(pltpu.roll(pick, HOP * d, 1) if d else pick)
        last = []
        for j in range(4):
            wide = turned[(-j) % 4]
            for b in (1, 2, 3):
                wide = jnp.where(quarter == b, turned[(b - j) % 4], wide)
            lower = jnp.concatenate([above[j], wide[:-8]], axis=0)
            side[j, 16 + low : 16 + low + ROWS, :] = jnp.concatenate([wide, lower], axis=1).astype(BF16)
            last.append(wide[-8:])
        return last

    def product(c, s):
        toe, side = toes[c % 2], sides[c % 2]
        count = 2 * s + 2
        left = []
        for j in range(4):
            starts = [16 + ROWS * s - 16 * g for g in range(count)]
            left.append(jnp.concatenate([side[j, i : i + ROWS, :] for i in starts], axis=1))
        return jnp.dot(
            jnp.concatenate(left, axis=0), toe[: STEP * count, :], preferred_element_type=F32
        )

    def overlap_add(c, s, part):
        low = ROWS * s
        late = slice(7 + low, 7 + low + ROWS)
        same, carried = None, jnp.zeros((ROWS, LANES), F32)
        for j in range(4):
            span = slice(ROWS * j, ROWS * (j + 1))
            far_pad[j, 8 + low : 8 + low + ROWS, :] = part[span, LANES:]
            total = part[span, :LANES] + far_pad[j, late, :]
            if j == 0:
                same = total
                continue
            total = pltpu.roll(total, HOP * j, 1)
            wrapped = quarter < j
            same = same + jnp.where(wrapped, 0.0, total)
            carried = carried + jnp.where(wrapped, total, 0.0)
        s_pad[8 + low : 8 + low + ROWS, :] = carried
        own = pl.ds(GROUP * low + c, ROWS, stride=GROUP)
        y_all[own, :] = same + s_pad[late, :] + rows_ref[c : c + 1, :] * x_all[own, :]

    steps = LANES // ROWS
    nothing = [jnp.zeros((8, LANES), F32)] * 4
    fetch(0)
    above = nothing
    for s in range(steps):
        above = build_side(0, s, above)
        build_toe(0, s)
    pending = None
    for c in range(GROUP):
        if c + 1 < GROUP:
            fetch(c + 1)
        above = nothing
        for s in range(steps):
            if c + 1 < GROUP:
                above = build_side(c + 1, s, above)
                build_toe(c + 1, s)
            if pending is not None:
                overlap_add(*pending)
            pending = (c, s, product(c, s))
    overlap_add(*pending)
    summed = y_all[...].reshape(out_ref.shape)
    out_ref[...] = jnp.stack([summed[d] for d in RETURN_ORDER]).astype(BF16)


def gate_kernel(back_ref, gate_ref, rows_ref, energy_ref, out_ref):
    owners, rows, _ = back_ref.shape
    blocks = rows // GROUP
    values = back_ref[...].astype(F32)
    values = jnp.stack([values[RETURN_ORDER.index(d)] for d in range(owners)])
    values = values.reshape(owners, blocks, GROUP, LANES)
    own = jnp.sum(jnp.sum(values * values, axis=0), axis=1)
    for i in range(energy_ref.shape[0]):
        energy_ref[i] = own
    for a in range(blocks):
        block = values[:, a].reshape(owners * GROUP, LANES)
        span = slice(a * LANES, (a + 1) * LANES)
        for b in range(block.shape[0] // LANES):
            part = slice(b * LANES, (b + 1) * LANES)
            gain = rows_ref[GROUP + b : GROUP + b + 1, :]
            out_ref[span, part] = gate_ref[span, part].astype(F32) * block[part, :].T * gain


def scale_kernel(channels, gated_ref, energy_ref, out_ref, staged, sem):
    energy = jnp.sum(energy_ref[...], axis=0)
    scale = lax.rsqrt(energy / channels + EPSILON)
    stores = []
    for a in range(scale.shape[0]):
        column = jnp.broadcast_to(scale[a : a + 1, :], (LANES, LANES)).T
        span = slice(a * LANES, (a + 1) * LANES)
        for b in range(0, staged.shape[1], LANES):
            staged[span, b : b + LANES] = (gated_ref[span, b : b + LANES] * column).astype(BF16)
        store = pltpu.make_async_copy(staged.at[span, :], out_ref.at[span, :], sem.at[a])
        store.start()
        stores.append(store)
    for store in stores:
        store.wait()


def per_device(gate_in, key_in, value_in, filters, skip, gain):
    rows, channels = key_in.shape
    ctx = lax.axis_size("ctx")
    tp = lax.axis_size("tp")
    blocks = rows // LANES
    here = blocks * GROUP
    params = pltpu.CompilerParams(vmem_limit_bytes=32 * 1024 * 1024)
    packed, small = pl.pallas_call(
        pack_kernel,
        out_shape=[
            jax.ShapeDtypeStruct((ctx, 2 * here, LANES), BF16),
            jax.ShapeDtypeStruct((GROUP + channels // LANES, LANES), F32),
        ],
        in_specs=[pl.BlockSpec(memory_space=pltpu.SMEM)] + [anywhere()] * 5,
        out_specs=[whole()] * 2,
        scratch_shapes=[pltpu.VMEM((rows, channels), BF16)] * 3
        + [pltpu.SMEM((channels,), F32), pltpu.SemaphoreType.DMA((5,))],
        compiler_params=params,
        name="pack",
    )(
        lax.axis_index("ctx").reshape(1),
        *(pltpu.with_memory_space_constraint(v, pltpu.HBM) for v in (key_in, value_in, filters, skip)),
        pltpu.with_memory_space_constraint(gain.reshape(-1, LANES), pltpu.HBM),
    )
    recv = lax.all_to_all(
        packed, "ctx", split_axis=0, concat_axis=0, tiled=True, axis_index_groups=[SEND_ORDER]
    )
    summed = pl.pallas_call(
        conv_kernel,
        out_shape=jax.ShapeDtypeStruct((ctx, here, LANES), BF16),
        in_specs=[whole()] * 2,
        out_specs=whole(),
        scratch_shapes=[pltpu.VMEM((ctx * here, LANES), F32)] * 3
        + [
            pltpu.VMEM((8 + LANES, LANES), F32),
            pltpu.VMEM((8 + LANES, LANES), F32),
            pltpu.VMEM((8 + LANES, LANES), F32),
            pltpu.VMEM((4, 8 + LANES, LANES), F32),
            pltpu.VMEM((LANES // 2 * HOP, STEP), BF16),
            pltpu.VMEM((LANES // 2 * HOP, STEP), BF16),
            pltpu.VMEM((4, 16 + LANES, STEP), BF16),
            pltpu.VMEM((4, 16 + LANES, STEP), BF16),
        ],
        compiler_params=params,
        name="conv",
    )(recv, small)
    back = lax.all_to_all(
        summed, "ctx", split_axis=0, concat_axis=0, tiled=True, axis_index_groups=[RETURN_ORDER]
    )
    own, gated = pl.pallas_call(
        gate_kernel,
        out_shape=[
            jax.ShapeDtypeStruct((tp, blocks, LANES), F32),
            jax.ShapeDtypeStruct((rows, channels), F32),
        ],
        in_specs=[whole()] * 3,
        out_specs=[whole()] * 2,
        compiler_params=params,
        name="gate",
    )(back, gate_in, small)
    energy = lax.all_to_all(own, "tp", split_axis=0, concat_axis=0, tiled=True)
    return pl.pallas_call(
        functools.partial(scale_kernel, channels * tp),
        out_shape=jax.ShapeDtypeStruct((rows, channels), BF16),
        in_specs=[whole()] * 2,
        out_specs=anywhere(),
        scratch_shapes=[pltpu.VMEM((rows, channels), BF16), pltpu.SemaphoreType.DMA((blocks,))],
        compiler_params=params,
        name="scale",
    )(gated, energy)


def solution(mesh):
    in_specs = (P("ctx", "tp"), P("ctx", "tp"), P("ctx", "tp"), P("ctx", "tp"), P("tp"), P("tp"))
    out_specs = P("ctx", "tp")
    return jax.shard_map(
        per_device, mesh=mesh, in_specs=in_specs, out_specs=out_specs, check_vma=False
    )
```

```python
import functools

import jax
import jax.numpy as jnp
from jax import lax
from jax.experimental import pallas as pl
from jax.experimental.pallas import tpu as pltpu
from jax.sharding import PartitionSpec as P

EPSILON = 1e-05
LANES = 128
GROUP = 8
HOP = 32
STEP = 256
ROWS = 32
SEND_ORDER = [8 * x + (2 * x + y) % 8 for y in range(8) for x in range(4)]
RETURN_ORDER = [8 * x + y for y in (0, 4, 1, 5, 2, 6, 3, 7) for x in (0, 2, 1, 3)]
F32 = jnp.float32
BF16 = jnp.bfloat16


def whole():
    return pl.BlockSpec(memory_space=pltpu.VMEM)


def anywhere():
    return pl.BlockSpec(memory_space=pl.ANY)


def anywhere():
    return pl.BlockSpec(memory_space=pltpu.HBM)


def flip_blocks(rows):
    parts = []
    for a in range(rows.shape[0] // LANES):
        block = rows[a * LANES : (a + 1) * LANES, :].T
        parts.append(block.reshape(block.shape[0] // GROUP, GROUP, LANES))
    owners = jnp.concatenate(parts, axis=1)
    return jnp.stack([owners[d] for d in SEND_ORDER])


def pack_kernel(
    place_ref, key_ref, value_ref, taps_ref, skip_ref, gain_ref, out_ref, rows_ref, key, value, taps, skip, in_sem
):
    half = out_ref.shape[1] // 2
    gain = rows_ref.at[GROUP:, :]
    loads = []
    pairs = ((taps_ref, taps), (key_ref, key), (value_ref, value), (skip_ref, skip), (gain_ref, gain))
    for i, (src, dst) in enumerate(pairs):
        load = pltpu.make_async_copy(src, dst, in_sem.at[i])
        load.start()
        loads.append(load)
    loads[0].wait()
    out_ref[:, half:, :] = flip_blocks(taps[...].astype(F32)).astype(BF16)
    loads[1].wait()
    loads[2].wait()
    mixed = key[...].astype(F32) * value[...].astype(F32)
    out_ref[:, :half, :] = flip_blocks(mixed).astype(BF16)
    loads[3].wait()
    loads[4].wait()
    for c in range(GROUP):
        rows_ref[c : c + 1, :] = jnp.full((1, LANES), skip[place_ref[0] * GROUP + c], F32)


def conv_kernel(
    recv_ref, rows_ref, out_ref, x_all, h_all, y_all, x_pad, h_pad, s_pad, far_pad, toe_0, toe_1, side_0, side_1
):
    owners, both, _ = recv_ref.shape
    half = both // 2
    for i, d in enumerate(SEND_ORDER):
        x_all[d * half : (d + 1) * half, :] = recv_ref[i, :half, :].astype(F32)
        h_all[d * half : (d + 1) * half, :] = recv_ref[i, half:, :].astype(F32)
    x_pad[:8, :] = jnp.zeros((8, LANES), F32)
    h_pad[:8, :] = jnp.zeros((8, LANES), F32)
    s_pad[:8, :] = jnp.zeros((8, LANES), F32)
    far_pad[:, :8, :] = jnp.zeros((4, 8, LANES), F32)
    toes = (toe_0, toe_1)
    sides = (side_0, side_1)
    for side in sides:
        side[:, :16, :] = jnp.zeros((4, 16, STEP), BF16)
    lane = lax.broadcasted_iota(jnp.int32, (8, LANES), 1)
    row = lax.broadcasted_iota(jnp.int32, (8, LANES), 0)
    edge = lane + row
    quarter = lax.broadcasted_iota(jnp.int32, (ROWS, LANES), 1) // HOP

    def fetch(c):
        h_pad[8:, :] = h_all[pl.ds(c, LANES, stride=GROUP), :]
        x_pad[8:, :] = x_all[pl.ds(c, LANES, stride=GROUP), :]

    def build_toe(c, s):
        toe = toes[c % 2]
        for k in range(ROWS * s, ROWS * (s + 1)):
            now = jnp.broadcast_to(h_pad[8 + k : 9 + k, :], (8, LANES))
            before = jnp.broadcast_to(h_pad[7 + k : 8 + k, :], (8, LANES))
            tiles = []
            for v in range(0, HOP, 8):
                source = jnp.where(edge >= LANES - v, before, now)
                tiles.append(pltpu.roll(source, v, 1, stride=1, stride_axis=0))
            toe[k // 2 * HOP : (k // 2 + 1) * HOP, k % 2 * LANES : (k % 2 + 1) * LANES] = (
                jnp.concatenate(tiles, axis=0).astype(BF16)
            )

    def build_side(c, s, above):
        side = sides[c % 2]
        low = ROWS * s
        late = [x_pad[8 - 2 * b + low : 8 - 2 * b + low + ROWS, :] for b in range(4)]
        turned = []
        for d in range(4):
            pick = late[d]
            for j in (1, 2, 3):
                pick = jnp.where(quarter == j, late[(j + d) % 4], pick)
            turned.append(pltpu.roll(pick, HOP * d, 1) if d else pick)
        last = []
        for j in range(4):
            wide = turned[(-j) % 4]
            for b in (1, 2, 3):
                wide = jnp.where(quarter == b, turned[(b - j) % 4], wide)
            lower = jnp.concatenate([above[j], wide[:-8]], axis=0)
            side[j, 16 + low : 16 + low + ROWS, :] = jnp.concatenate([wide, lower], axis=1).astype(BF16)
            last.append(wide[-8:])
        return last

    def product(c, s):
        toe, side = toes[c % 2], sides[c % 2]
        count = 2 * s + 2
        left = []
        for j in range(4):
            starts = [16 + ROWS * s - 16 * g for g in range(count)]
            left.append(jnp.concatenate([side[j, i : i + ROWS, :] for i in starts], axis=1))
        return jnp.dot(
            jnp.concatenate(left, axis=0), toe[: STEP * count, :], preferred_element_type=F32
        )

    def overlap_add(c, s, part):
        low = ROWS * s
        late = slice(7 + low, 7 + low + ROWS)
        same, carried = None, jnp.zeros((ROWS, LANES), F32)
        for j in range(4):
            span = slice(ROWS * j, ROWS * (j + 1))
            far_pad[j, 8 + low : 8 + low + ROWS, :] = part[span, LANES:]
            total = part[span, :LANES] + far_pad[j, late, :]
            if j == 0:
                same = total
                continue
            total = pltpu.roll(total, HOP * j, 1)
            wrapped = quarter < j
            same = same + jnp.where(wrapped, 0.0, total)
            carried = carried + jnp.where(wrapped, total, 0.0)
        s_pad[8 + low : 8 + low + ROWS, :] = carried
        own = pl.ds(GROUP * low + c, ROWS, stride=GROUP)
        y_all[own, :] = same + s_pad[late, :] + rows_ref[c : c + 1, :] * x_all[own, :]

    steps = LANES // ROWS
    nothing = [jnp.zeros((8, LANES), F32)] * 4
    fetch(0)
    above = nothing
    for s in range(steps):
        above = build_side(0, s, above)
        build_toe(0, s)
    pending = []
    for c in range(GROUP):
        if c + 1 < GROUP:
            fetch(c + 1)
        above = nothing
        for s in range(steps):
            if c + 1 < GROUP:
                above = build_side(c + 1, s, above)
                build_toe(c + 1, s)
            if len(pending) == 2:
                overlap_add(*pending.pop(0))
            pending.append((c, s, product(c, s)))
    for late in pending:
        overlap_add(*late)
    summed = y_all[...].reshape(out_ref.shape)
    out_ref[...] = jnp.stack([summed[d] for d in RETURN_ORDER]).astype(BF16)


def gate_kernel(back_ref, gate_ref, rows_ref, energy_ref, out_ref):
    owners, rows, _ = back_ref.shape
    blocks = rows // GROUP
    values = back_ref[...].astype(F32)
    values = jnp.stack([values[RETURN_ORDER.index(d)] for d in range(owners)])
    values = values.reshape(owners, blocks, GROUP, LANES)
    own = jnp.sum(jnp.sum(values * values, axis=0), axis=1)
    for i in range(energy_ref.shape[0]):
        energy_ref[i] = own
    for a in range(blocks):
        block = values[:, a].reshape(owners * GROUP, LANES)
        span = slice(a * LANES, (a + 1) * LANES)
        for b in range(block.shape[0] // LANES):
            part = slice(b * LANES, (b + 1) * LANES)
            gain = rows_ref[GROUP + b : GROUP + b + 1, :]
            out_ref[span, part] = gate_ref[span, part].astype(F32) * block[part, :].T * gain


def scale_kernel(channels, gated_ref, energy_ref, out_ref, staged, sem):
    energy = jnp.sum(energy_ref[...], axis=0)
    scale = lax.rsqrt(energy / channels + EPSILON)
    stores = []
    for a in range(scale.shape[0]):
        column = jnp.broadcast_to(scale[a : a + 1, :], (LANES, LANES)).T
        span = slice(a * LANES, (a + 1) * LANES)
        for b in range(0, staged.shape[1], LANES):
            staged[span, b : b + LANES] = (gated_ref[span, b : b + LANES] * column).astype(BF16)
        store = pltpu.make_async_copy(staged.at[span, :], out_ref.at[span, :], sem.at[a])
        store.start()
        stores.append(store)
    for store in stores:
        store.wait()


def per_device(gate_in, key_in, value_in, filters, skip, gain):
    rows, channels = key_in.shape
    ctx = lax.axis_size("ctx")
    tp = lax.axis_size("tp")
    blocks = rows // LANES
    here = blocks * GROUP
    params = pltpu.CompilerParams(vmem_limit_bytes=32 * 1024 * 1024)
    packed, small = pl.pallas_call(
        pack_kernel,
        out_shape=[
            jax.ShapeDtypeStruct((ctx, 2 * here, LANES), BF16),
            jax.ShapeDtypeStruct((GROUP + channels // LANES, LANES), F32),
        ],
        in_specs=[pl.BlockSpec(memory_space=pltpu.SMEM)] + [anywhere()] * 5,
        out_specs=[whole()] * 2,
        scratch_shapes=[pltpu.VMEM((rows, channels), BF16)] * 3
        + [pltpu.SMEM((channels,), F32), pltpu.SemaphoreType.DMA((5,))],
        compiler_params=params,
        name="pack",
    )(
        lax.axis_index("ctx").reshape(1),
        *(pltpu.with_memory_space_constraint(v, pltpu.HBM) for v in (key_in, value_in, filters, skip)),
        pltpu.with_memory_space_constraint(gain.reshape(-1, LANES), pltpu.HBM),
    )
    recv = lax.all_to_all(
        packed, "ctx", split_axis=0, concat_axis=0, tiled=True, axis_index_groups=[SEND_ORDER]
    )
    summed = pl.pallas_call(
        conv_kernel,
        out_shape=jax.ShapeDtypeStruct((ctx, here, LANES), BF16),
        in_specs=[whole()] * 2,
        out_specs=whole(),
        scratch_shapes=[pltpu.VMEM((ctx * here, LANES), F32)] * 3
        + [
            pltpu.VMEM((8 + LANES, LANES), F32),
            pltpu.VMEM((8 + LANES, LANES), F32),
            pltpu.VMEM((8 + LANES, LANES), F32),
            pltpu.VMEM((4, 8 + LANES, LANES), F32),
            pltpu.VMEM((LANES // 2 * HOP, STEP), BF16),
            pltpu.VMEM((LANES // 2 * HOP, STEP), BF16),
            pltpu.VMEM((4, 16 + LANES, STEP), BF16),
            pltpu.VMEM((4, 16 + LANES, STEP), BF16),
        ],
        compiler_params=params,
        name="conv",
    )(recv, small)
    back = lax.all_to_all(
        summed, "ctx", split_axis=0, concat_axis=0, tiled=True, axis_index_groups=[RETURN_ORDER]
    )
    own, gated = pl.pallas_call(
        gate_kernel,
        out_shape=[
            jax.ShapeDtypeStruct((tp, blocks, LANES), F32),
            jax.ShapeDtypeStruct((rows, channels), F32),
        ],
        in_specs=[whole()] * 3,
        out_specs=[whole()] * 2,
        compiler_params=params,
        name="gate",
    )(back, gate_in, small)
    energy = lax.all_to_all(own, "tp", split_axis=0, concat_axis=0, tiled=True)
    return pl.pallas_call(
        functools.partial(scale_kernel, channels * tp),
        out_shape=jax.ShapeDtypeStruct((rows, channels), BF16),
        in_specs=[whole()] * 2,
        out_specs=anywhere(),
        scratch_shapes=[pltpu.VMEM((rows, channels), BF16), pltpu.SemaphoreType.DMA((blocks,))],
        compiler_params=params,
        name="scale",
    )(gated, energy)


def solution(mesh):
    in_specs = (P("ctx", "tp"), P("ctx", "tp"), P("ctx", "tp"), P("ctx", "tp"), P("tp"), P("tp"))
    out_specs = P("ctx", "tp")
    return jax.shard_map(
        per_device, mesh=mesh, in_specs=in_specs, out_specs=out_specs, check_vma=False
    )
```
